256 devices in a mesh: row: 16 (over z, core), col: 16 (over y, x).
Axes of the slice: x: 4, y: 4, z: 8, core: 2. Of those that a mesh axis runs over, the one named last changes fastest.
Arguments:
- density: bfloat16 [256, 16, 4096], P('row', 'col'), may hold values from -1 to 2, as said below
- columns: int32 [256, 16], P('row', 'col'), may hold values from 0 to 255, as said below
Outputs:
- purified: bfloat16 [256, 16, 4096], P('row', 'col')
The draws below stay inside these ranges and needn't reach their ends.
Inputs may be any that keep to these rules, and one draw needn't show every extreme that they name: In each block row and each group g of 16 block columns (g * 16 to (g + 1) * 16 - 1), the slots g * 1 to (g + 1) - 1 list 1 different block columns of that group; the block row's own diagonal block is listed, in the first slot of its group; the pattern is symmetric: block column j is listed in block row i exactly when block column i is listed in block row j. full(density) is symmetric: the listed block (j, i) is the transpose of the listed block (i, j), and diagonal blocks are symmetric; the diagonal block of a block row also carries occupations between 0 and 1 on its diagonal.
All inputs are finite; a program needn't handle non-finite values.
Results may differ from the reference program's by a relative error of at most 0.01.
Values may be sent and summed in bfloat16 or wider, within the bound.
No kernel may reach another device: no remote copies, remote signals or barrier semaphores. Data moves between devices by JAX's collectives and lax.ppermute only.
A program may use at most 64 MiB of HBM per device.

```python
import jax
import jax.numpy as jnp
from jax import lax

BS = 64
SLOTS = 1
STEPS = 2
NBLOCKS = 256
GROUP_COLS = 16
LISTED = 16
N_COL = 16


def block_pattern(key):
    width = GROUP_COLS
    perm_keys = jax.random.split(jax.random.fold_in(key, 1), N_COL)
    places = jax.vmap(lambda sub: jax.random.permutation(sub, width))(perm_keys).astype(jnp.int32)
    inverse = jnp.argsort(places, axis=1).astype(jnp.int32)
    raw_shift = jax.random.randint(jax.random.fold_in(key, 2), (N_COL, N_COL), 0, width).astype(jnp.int32)
    shifts = (raw_shift - raw_shift.T) % width
    block_ids = jnp.arange(NBLOCKS, dtype=jnp.int32)
    home = block_ids // width
    local = block_ids % width
    slot_ids = jnp.arange(SLOTS, dtype=jnp.int32)
    offsets = (slot_ids + 1) // 2 * jnp.where(slot_ids % 2 == 1, 1, -1).astype(jnp.int32)
    own_place = places[home, local]
    target = (own_place[:, None, None] - shifts[home][:, :, None] + offsets[None, None, :]) % width
    group_ids = jnp.arange(N_COL, dtype=jnp.int32)
    chosen = inverse[group_ids[None, :, None], target]
    picked = chosen + (group_ids * width)[None, :, None]
    return picked.reshape(NBLOCKS, LISTED).astype(jnp.int32)


def draw_columns(key, part):
    return block_pattern(jax.random.fold_in(key, 7))


def draw_density(key, part):
    columns = block_pattern(jax.random.fold_in(key, 7))
    sigma = 0.8 / (BS * LISTED) ** 0.5
    noise_key = jax.random.fold_in(key, 11)
    occ_key = jax.random.fold_in(key, 12)
    row_ids = jnp.broadcast_to(jnp.arange(NBLOCKS, dtype=jnp.int32)[:, None], (NBLOCKS, LISTED)).reshape(-1)
    col_ids = columns.reshape(-1)
    lower = jnp.minimum(row_ids, col_ids)
    upper = jnp.maximum(row_ids, col_ids)

    def one_block(first, second, row_id, col_id):
        sub = jax.random.fold_in(noise_key, first * NBLOCKS + second)
        noise = jax.random.normal(sub, (BS, BS), jnp.float32)
        turned = jnp.where(row_id > col_id, noise.T, noise)
        return jnp.where(row_id == col_id, (noise + noise.T) * 0.70710678, turned)
    noise = jax.vmap(one_block)(lower, upper, row_ids, col_ids).reshape(NBLOCKS, LISTED, BS, BS)
    occupied = jax.random.uniform(occ_key, (NBLOCKS, 1, BS, 1), jnp.float32)
    block_ids = jnp.arange(NBLOCKS, dtype=jnp.int32)
    diagonal_slot = (block_ids // GROUP_COLS * SLOTS)[:, None] == jnp.arange(LISTED, dtype=jnp.int32)[None, :]
    identity = (jnp.arange(BS)[:, None] == jnp.arange(BS)[None, :]).astype(jnp.float32)
    values = sigma * noise + jnp.where(diagonal_slot[:, :, None, None], occupied * identity[None, None, :, :], 0.0)
    return values.reshape(NBLOCKS, LISTED, BS * BS).astype(jnp.bfloat16)


def setup_inputs(seed: int = 0) -> dict:
    splits = jax.random.split(jax.random.key(seed), 3)
    return {
        "density": draw_density(jax.random.fold_in(splits[2], 71), 0),
        "columns": draw_columns(jax.random.fold_in(splits[2], 71), 0),
    }


def densify(blocks, columns):
    rows = jnp.arange(NBLOCKS, dtype=jnp.int32)[:, None]
    grid = jnp.zeros((NBLOCKS, NBLOCKS, BS, BS), jnp.float32)
    grid = grid.at[rows, columns].set(blocks.astype(jnp.float32).reshape(NBLOCKS, LISTED, BS, BS))
    return grid.transpose(0, 2, 1, 3).reshape(NBLOCKS * BS, NBLOCKS * BS)


def listed_blocks(matrix, columns):
    rows = jnp.arange(NBLOCKS, dtype=jnp.int32)[:, None]
    grid = matrix.reshape(NBLOCKS, BS, NBLOCKS, BS).transpose(0, 2, 1, 3)
    return grid[rows, columns].reshape(NBLOCKS, LISTED, BS * BS)


def reference(density, columns):
    current = density
    for iteration in range(STEPS):
        dense_now = densify(current, columns)
        squared = listed_blocks(jnp.dot(dense_now, dense_now, precision=lax.Precision.HIGHEST, preferred_element_type=jnp.float32), columns).astype(jnp.bfloat16)
        dense_sq = densify(squared, columns)
        cubed = listed_blocks(jnp.dot(dense_sq, dense_now, precision=lax.Precision.HIGHEST, preferred_element_type=jnp.float32), columns)
        current = (3.0 * squared.astype(jnp.float32) - 2.0 * cubed).astype(jnp.bfloat16)
    return current
```

```python
import functools

import jax
import jax.numpy as jnp
import numpy as np
from jax import lax
from jax.experimental import pallas as pl
from jax.experimental.pallas import tpu as pltpu
from jax.sharding import PartitionSpec as P

STEPS = 2
SIDE = 64
HALF = 8
ROWS = 32
PIECE = HALF * ROWS + 16
BF16 = jnp.bfloat16


def shuffle_matrix():
    m = np.zeros((128, 128), np.float32)
    for lane in range(128):
        q, y = divmod(lane, SIDE)
        m[lane, 64 * q + 32 * (y % 2) + y // 2] = 1.0
    return m


def col_shift(dy, dx):
    return [(y * 4 + x, ((y + dy) % 4) * 4 + (x + dx) % 4) for y in range(4) for x in range(4)]


def z_shift(d):
    return [(z * 2 + c, ((z + d) % 8) * 2 + c) for z in range(8) for c in range(2)]


CORES = [(i, i ^ 1) for i in range(16)]


def gather_left(half0, half1):
    first = [half0] + [lax.ppermute(half0, "col", col_shift(0, d)) for d in (1, 2, 3)]
    other = [half1] + [lax.ppermute(half1, "col", col_shift(d, 0)) for d in (1, 2, 3)]
    first = jnp.concatenate(first, axis=0)
    other = jnp.concatenate(other, axis=0)
    first = [first] + [lax.ppermute(first, "col", col_shift(d, 0)) for d in (1, 2, 3)]
    other = [other] + [lax.ppermute(other, "col", col_shift(0, d)) for d in (1, 2, 3)]
    return first, other


def gather_right(half0, half1):
    mine = jnp.concatenate([half0, half1], axis=0)
    own = [mine] + [lax.ppermute(mine, "row", z_shift(d)) for d in range(1, 8)]
    own = jnp.concatenate(own, axis=0)
    return own, lax.ppermute(own, "row", CORES)


def products(table, lefts, rights, acc):
    acc[...] = jnp.zeros_like(acc)
    low = lax.broadcasted_iota(jnp.int32, (ROWS, 128), 1) < SIDE
    for h in range(2):
        for s in range(16):
            found = functools.reduce(jnp.maximum, [table[h, s, i] for i in range(HALF)])

            @pl.when(found >= 0)
            def _(h=h, s=s):
                left = lefts[h][s // 4]
                for i in range(HALF):
                    at = table[h, s, i]
                    row = pl.multiple_of(jnp.maximum(at, 0), 16)
                    block = rights[pl.ds(row, ROWS), :]
                    block = jnp.where(at >= 0, block, jnp.zeros_like(block))
                    turned = jnp.concatenate([block[:, SIDE:], block[:, :SIDE]], axis=1)
                    zero = jnp.zeros_like(block)
                    weights = jnp.concatenate(
                        [
                            jnp.where(low, block, zero),
                            jnp.where(low, turned, zero),
                            jnp.where(low, zero, turned),
                            jnp.where(low, zero, block),
                        ],
                        axis=0,
                    )
                    base = (s % 4) * PIECE + i * ROWS
                    out = pl.ds((h * HALF + i) * ROWS, ROWS)
                    acc[out, :] += jnp.dot(
                        left[base : base + ROWS, :], weights, preferred_element_type=jnp.float32
                    )


def write_halves(value, shuffle, plain, mixed):
    turned = jnp.dot(value, shuffle[...], preferred_element_type=jnp.float32).astype(BF16)
    for h in range(2):
        part = slice(h * HALF * ROWS, (h + 1) * HALF * ROWS)
        for refs, whole in ((plain, value), (mixed, turned)):
            if refs is not None:
                refs[h][: HALF * ROWS, :] = whole[part, :]
                refs[h][HALF * ROWS :, :] = jnp.zeros((16, 128), BF16)


def square_kernel(table, shuffle, *refs):
    lefts, rights = (refs[0:4], refs[4:8]), refs[8]
    squared, mixed, acc = refs[9], refs[10:12], refs[12]
    products(table, lefts, rights, acc)
    value = acc[...].astype(BF16)
    squared[...] = value
    write_halves(value, shuffle, None, mixed)


def cube_kernel(last, table, shuffle, *refs):
    lefts, rights, squared = (refs[0:4], refs[4:8]), refs[8], refs[9]
    products(table, lefts, rights, refs[-1])
    value = (3.0 * squared[...].astype(jnp.float32) - 2.0 * refs[-1][...]).astype(BF16)
    if last:
        refs[10][...] = value
    else:
        write_halves(value, shuffle, refs[10:12], refs[12:14])


def call(kernel, outs, *args):
    vmem = pl.BlockSpec(memory_space=pltpu.VMEM)
    return pl.pallas_call(
        kernel,
        out_shape=outs,
        in_specs=[pl.BlockSpec(memory_space=pltpu.SMEM)] + [vmem] * (len(args) - 1),
        out_specs=[vmem] * len(outs),
        scratch_shapes=[pltpu.VMEM((16 * ROWS, 128), jnp.float32)],
        compiler_params=pltpu.CompilerParams(vmem_limit_bytes=32 * 1024 * 1024),
    )(*args)


WHOLE = jax.ShapeDtypeStruct((16 * ROWS, 128), BF16)
PART = jax.ShapeDtypeStruct((PIECE, 128), BF16)


def with_columns(blocks, columns):
    pieces = []
    for h in range(2):
        tag = columns[h * HALF : (h + 1) * HALF].astype(BF16)
        tag = jnp.pad(tag[None, :], ((0, 15), (0, 128 - HALF)))
        pieces.append(jnp.concatenate([blocks[h * HALF * ROWS : (h + 1) * HALF * ROWS], tag], axis=0))
    return pieces


def tags(panel):
    return panel.reshape(-1, PIECE, 128)[:, HALF * ROWS, :HALF].astype(jnp.int32)


def match_table(columns, lefts, right):
    place = lax.axis_index("row")
    z, core = place // 2, place % 2
    listed = tags(right).reshape(256)
    result = []
    for h in range(2):
        block = jnp.concatenate([tags(p) for p in lefts[h]], axis=0)
        group, local = block // 16, block % 16
        piece = jnp.where(group % 2 == core, 0, 8) + (z - group // 2) % 8
        at = piece * 16 + local
        hit = at[:, :, None] == jnp.arange(256, dtype=jnp.int32)
        there = jnp.sum(jnp.where(hit, listed, 0), axis=2)
        row = piece * (2 * PIECE) + local // HALF * PIECE + local % HALF * ROWS
        result.append(jnp.where(there == columns[None, h * HALF : (h + 1) * HALF], row, -1))
    return jnp.stack(result)


def body(density, columns):
    shuffle = jnp.asarray(shuffle_matrix(), BF16)
    columns = columns.reshape(16)
    blocks = density.reshape(16 * ROWS, 128)
    turned = jnp.dot(blocks, shuffle, preferred_element_type=jnp.float32).astype(BF16)
    plain = with_columns(blocks, columns)
    mixed = with_columns(turned, columns)
    table = None
    for step in range(STEPS):
        last = step == STEPS - 1
        lefts = gather_left(*mixed)
        right = jnp.concatenate(gather_right(*plain), axis=0)
        if table is None:
            table = match_table(columns, lefts, right)
        squared, *mixed = call(
            square_kernel, [WHOLE, PART, PART], table, shuffle, *lefts[0], *lefts[1], right
        )
        lefts = gather_left(*mixed)
        done = call(
            functools.partial(cube_kernel, last),
            [WHOLE] if last else [PART] * 4,
            table,
            shuffle,
            *lefts[0],
            *lefts[1],
            right,
            squared,
        )
        plain, mixed = done[:2], done[2:]
    return done[0].reshape(16, 1, 4096)


def solution(mesh):
    placed = (P("row", "col", None), P("row", "col"))
    return jax.shard_map(
        body, mesh=mesh, in_specs=placed, out_specs=P("row", "col", None), check_vma=False
    )
```

```python
import jax
import jax.numpy as jnp
from jax import lax
from jax.experimental import pallas as pl
from jax.experimental.pallas import tpu as pltpu
from jax.sharding import PartitionSpec as P

STEPS = 2
SIDE = 64
ROWS = 32
TAG = 16
WHOLE = 16 * ROWS
BF16 = jnp.bfloat16
F32 = jnp.float32


def shift(first, d):
    pairs = []
    for row in range(16):
        for y in range(4):
            for x in range(4):
                along_x = (row % 2 == 0) == first
                to = (y, (x + d) % 4) if along_x else ((y + d) % 4, x)
                pairs.append((row * 16 + y * 4 + x, row * 16 + to[0] * 4 + to[1]))
    return pairs


def gather_left(own):
    near = [own] + [lax.ppermute(own, ("row", "col"), shift(True, d)) for d in (1, 3, 2)]
    near = jnp.concatenate(near, axis=0)
    return [near] + [lax.ppermute(near, ("row", "col"), shift(False, d)) for d in (1, 3, 2)]


def turn(value):
    at = lax.broadcasted_iota(jnp.int32, (128, 128), 0)
    to = lax.broadcasted_iota(jnp.int32, (128, 128), 1)
    place = at // 64 * 64 + at % 2 * 32 + at % 64 // 2
    shuffle = (place == to).astype(F32).astype(BF16)
    return jnp.dot(value, shuffle, preferred_element_type=F32).astype(BF16)


def prepare_kernel(density, columns, plain, mixed, blocks, note):
    wide = density[...].astype(F32)
    for p in range(ROWS):
        blocks[pl.ds(p, 16, stride=ROWS), :] = wide[:, 128 * p : 128 * (p + 1)]
    value = blocks[...].astype(BF16)
    note[...] = jnp.zeros_like(note)
    note[0:1, 0:16] = columns[...].astype(F32)
    tag = note[...].astype(BF16)
    plain[:WHOLE, :] = value
    plain[WHOLE:, :] = tag
    mixed[:WHOLE, :] = turn(value)
    mixed[WHOLE:, :] = tag


def products(table, pieces, right, acc):
    step = pieces[0].shape[0] // 4
    extra = right.shape[0] // 16 - WHOLE
    acc[...] = jnp.zeros_like(acc)
    low = lax.broadcasted_iota(jnp.int32, (ROWS, 128), 1) < SIDE
    zero = jnp.zeros((ROWS, 128), BF16)

    def weights(s, i):
        k = table[s, i]
        at = jnp.maximum(k, 0)
        row = pl.multiple_of(at * ROWS + (at // 16) * extra, 16)
        block = jnp.where(k >= 0, right[pl.ds(row, ROWS), :], zero)
        turned = jnp.concatenate([block[:, SIDE:], block[:, :SIDE]], axis=1)
        return [
            jnp.where(low, block, zero),
            jnp.where(low, turned, zero),
            jnp.where(low, zero, turned),
            jnp.where(low, zero, block),
        ]

    def left(s, i):
        base = (s % 4) * step + i * ROWS
        return pieces[s // 4][base : base + ROWS, :]

    def add(slots):
        for i in range(16):
            a = [left(s, i) for s in slots]
            b = [w for s in slots for w in weights(s, i)]
            a = a[0] if len(a) == 1 else jnp.concatenate(a, axis=1)
            out = slice(i * ROWS, (i + 1) * ROWS)
            acc[out, :] += jnp.dot(a, jnp.concatenate(b, axis=0), preferred_element_type=F32)

    for g in range(4):
        slots = range(4 * g, 4 * g + 4)
        count = table[4 * g, 17]

        @pl.when(count > 1)
        def _(slots=slots):
            add(slots)

        @pl.when(count == 1)
        def _(slots=slots):
            for s in slots:

                @pl.when(table[s, 16] >= 0)
                def _(s=s):
                    add([s])


def square_kernel(table, p0, p1, p2, p3, right, squared, mixed, acc):
    products(table, (p0, p1, p2, p3), right, acc)
    value = acc[...].astype(BF16)
    squared[...] = value
    mixed[...] = turn(value)


def purify(table, p0, p1, p2, p3, right, squared, acc):
    products(table, (p0, p1, p2, p3), right, acc)
    return (3.0 * squared[...].astype(F32) - 2.0 * acc[...]).astype(BF16)


def cube_kernel(table, p0, p1, p2, p3, right, squared, plain, mixed, acc):
    value = purify(table, p0, p1, p2, p3, right, squared, acc)
    plain[...] = value
    mixed[...] = turn(value)


def last_kernel(table, p0, p1, p2, p3, right, squared, out, acc):
    acc[...] = purify(table, p0, p1, p2, p3, right, squared, acc).astype(F32)
    for p in range(ROWS):
        out[:, 128 * p : 128 * (p + 1)] = acc[pl.ds(p, 16, stride=ROWS), :].astype(BF16)


def shape(rows, lanes=128):
    return jax.ShapeDtypeStruct((rows, lanes), BF16)


VMEM = pl.BlockSpec(memory_space=pltpu.VMEM)
SMEM = pl.BlockSpec(memory_space=pltpu.SMEM)


def call(kernel, outs, specs, scratch, args):
    return pl.pallas_call(
        kernel,
        out_shape=outs,
        in_specs=specs,
        out_specs=[VMEM] * len(outs),
        scratch_shapes=[pltpu.VMEM((WHOLE, 128), F32)] + scratch,
        compiler_params=pltpu.CompilerParams(vmem_limit_bytes=24 * 1024 * 1024),
        cost_estimate=pl.CostEstimate(flops=2**31, bytes_accessed=2**21, transcendentals=0),
    )(*args)


def multiply(kernel, outs, table, pieces, *others):
    specs = [SMEM] + [VMEM] * (4 + len(others))
    return call(kernel, outs, specs, [], (table, *pieces, *others))


def tags(panel):
    return panel.reshape(16, WHOLE + TAG, 128)[:, WHOLE, :16].astype(jnp.int32)


def match_table(columns, pieces, right):
    listed = tags(right).reshape(256)
    block = tags(jnp.stack(pieces))
    hit = block[..., None] == jnp.arange(256, dtype=jnp.int32)
    there = jnp.sum(jnp.where(hit, listed, 0), axis=2)
    found = jnp.where(there == columns, block, -1)
    most = jnp.max(found, axis=1, keepdims=True)
    count = jnp.sum((most >= 0).astype(jnp.int32).reshape(4, 4), axis=1, keepdims=True)
    count = jnp.broadcast_to(count, (4, 4)).reshape(16, 1)
    return jnp.concatenate([found, most, count], axis=1)


def body(density, columns):
    columns = columns.reshape(1, 16)
    plain, mixed = call(
        prepare_kernel,
        [shape(WHOLE + TAG)] * 2,
        [VMEM, VMEM],
        [pltpu.VMEM((TAG, 128), F32)],
        (density.reshape(16, 4096), columns),
    )
    table = None
    for step in range(STEPS):
        right = lax.all_gather(plain, "row", axis=0, tiled=True)
        pieces = gather_left(mixed)
        if table is None:
            table = match_table(columns, pieces, right)
        outs = [shape(WHOLE)] * 2
        squared, mixed = multiply(square_kernel, outs, table, pieces, right)
        pieces = gather_left(mixed)
        if step < STEPS - 1:
            plain, mixed = multiply(cube_kernel, outs, table, pieces, right, squared)
    (out,) = multiply(last_kernel, [shape(16, 4096)], table, pieces, right, squared)
    return out.reshape(16, 1, 4096)


def solution(mesh):
    placed = (P("row", "col", None), P("row", "col"))
    return jax.shard_map(
        body, mesh=mesh, in_specs=placed, out_specs=P("row", "col", None), check_vma=False
    )
```

```python
import jax
import jax.numpy as jnp
from jax import lax
from jax.experimental import pallas as pl
from jax.experimental.pallas import tpu as pltpu
from jax.sharding import PartitionSpec as P

STEPS = 2
SIDE = 64
ROWS = 32
CHUNK = 8
TAG = 16
WHOLE = 16 * ROWS
BF16 = jnp.bfloat16
F32 = jnp.float32


def shift(first, d):
    pairs = []
    for row in range(16):
        for y in range(4):
            for x in range(4):
                along_x = (row % 2 == 0) == first
                to = (y, (x + d) % 4) if along_x else ((y + d) % 4, x)
                pairs.append((row * 16 + y * 4 + x, row * 16 + to[0] * 4 + to[1]))
    return pairs


def gather_left(own):
    near = [own] + [lax.ppermute(own, ("row", "col"), shift(True, d)) for d in (1, 3, 2)]
    near = jnp.concatenate(near, axis=0)
    return [near] + [lax.ppermute(near, ("row", "col"), shift(False, d)) for d in (1, 3, 2)]


def shift_z(d):
    pairs = []
    for row in range(16):
        up = d if row % 2 == 0 else -d
        to = (row // 2 + up) % 8 * 2 + row % 2
        pairs += [(row * 16 + c, to * 16 + c) for c in range(16)]
    return pairs


OTHER_CORE = [(row * 16 + c, (row ^ 1) * 16 + c) for row in range(16) for c in range(16)]


def join_kernel(one, two, own, a, b, c, near, second, half, taken):
    rows = own.shape[0]
    for i, part in enumerate((own, a, b, c)):
        near[i * rows : (i + 1) * rows, :] = part[...]
    second[...] = two[...]
    half[...] = two[:rows, :]
    taken[: 2 * rows, :] = one[...]
    taken[2 * rows :, :] = two[...]


def taken_kernel(first, three, four, taken):
    at = 0
    for part in (first, three, four):
        taken[at : at + part.shape[0], :] = part[...]
        at += part.shape[0]


def gather_both(plain, mixed):
    def send(value, pairs):
        return lax.ppermute(value, ("row", "col"), pairs)

    rows = plain.shape[0]
    near = [send(mixed, shift(True, d)) for d in (1, 3, 2)]
    pair = jnp.concatenate([plain, send(plain, OTHER_CORE)], axis=0)
    one, two = send(pair, shift_z(1)), send(pair, shift_z(2))
    near, two, half, taken = call(
        join_kernel,
        [shape(4 * rows), shape(2 * rows), shape(rows), shape(4 * rows)],
        [VMEM] * 6,
        [],
        (one, two, mixed, *near),
        False,
    )
    pieces = [near] + [send(near, shift(False, d)) for d in (1, 3, 2)]
    three, four = send(two, shift_z(1)), send(half, shift_z(2))
    three, four, *pieces[1:] = lax.optimization_barrier((three, four, *pieces[1:]))
    (taken,) = call(taken_kernel, [shape(7 * rows)], [VMEM] * 3, [], (taken, three, four), False)
    right = (pair, taken, send(taken, OTHER_CORE))
    return pieces, right


def place_of(block):
    row = lax.axis_index("row")
    z, core = row // 2, row % 2
    group = block // 16
    other = (group % 2 != core).astype(jnp.int32)
    far = jnp.where(core == 0, z - group // 2, group // 2 - z) % 8
    panel = jnp.where(
        far == 0,
        other,
        jnp.where(
            far < 4,
            2 * far + other,
            jnp.where(far == 4, 8 + 7 * other, 9 + 2 * (7 - far) + 1 - other),
        ),
    )
    return panel * 16 + block % 16


def turn(value):
    at = lax.broadcasted_iota(jnp.int32, (128, 128), 0)
    to = lax.broadcasted_iota(jnp.int32, (128, 128), 1)
    place = at // 64 * 64 + at % 2 * 32 + at % 64 // 2
    shuffle = (place == to).astype(F32).astype(BF16)
    return jnp.dot(value, shuffle, preferred_element_type=F32).astype(BF16)


def prepare_kernel(density, columns, plain, mixed, blocks, note):
    wide = density[...].astype(F32)
    for p in range(ROWS):
        blocks[pl.ds(p, 16, stride=ROWS), :] = wide[:, 128 * p : 128 * (p + 1)]
    value = blocks[...].astype(BF16)
    note[...] = jnp.zeros_like(note)
    note[0:1, 0:16] = columns[...].astype(F32)
    tag = note[...].astype(BF16)
    plain[:WHOLE, :] = value
    plain[WHOLE:, :] = tag
    mixed[:WHOLE, :] = turn(value)
    mixed[WHOLE:, :] = tag


def products(table, pieces, right, acc):
    step = pieces[0].shape[0] // 4
    acc[...] = jnp.zeros_like(acc)
    low = lax.broadcasted_iota(jnp.int32, (ROWS, 128), 1) < SIDE
    zero = jnp.zeros((ROWS, 128), BF16)

    def weights(s, i):
        at = table[s, i]
        row = pl.multiple_of(jnp.maximum(at, 0) * ROWS, 16)
        block = jnp.where(at >= 0, right[pl.ds(row, ROWS), :], zero)
        turned = jnp.concatenate([block[:, SIDE:], block[:, :SIDE]], axis=1)
        return [
            jnp.where(low, block, zero),
            jnp.where(low, turned, zero),
            jnp.where(low, zero, turned),
            jnp.where(low, zero, block),
        ]

    def add(g, places):
        def some(j, carry):
            for u in range(CHUNK):
                i = j * CHUNK + u
                rows = [pl.multiple_of(t * step + i * ROWS, 16) for t in places]
                a = [pieces[g][pl.ds(row, ROWS), :] for row in rows]
                b = [w for t in places for w in weights(4 * g + t, i)]
                a = a[0] if len(a) == 1 else jnp.concatenate(a, axis=1)
                out = pl.ds(pl.multiple_of(i * ROWS, 16), ROWS)
                acc[out, :] += jnp.dot(a, jnp.concatenate(b, axis=0), preferred_element_type=F32)
            return carry

        lax.fori_loop(0, 16 // CHUNK, some, 0)

    for g in range(4):
        count = table[4 * g, 17]

        @pl.when(count > 1)
        def _(g=g):
            add(g, range(4))

        @pl.when(count == 1)
        def _(g=g):
            def one(t, carry):
                @pl.when(table[4 * g + t, 16] >= 0)
                def _():
                    add(g, [t])

                return carry

            lax.fori_loop(0, 4, one, 0)


def square_kernel(table, p0, p1, p2, p3, pair, taken, other, right, squared, mixed, acc):
    panel = pair.shape[0] // 2
    place = 0
    for part in (pair, taken, other):
        for at in range(0, part.shape[0], panel):
            right[place : place + WHOLE, :] = part[at : at + WHOLE, :]
            place += WHOLE
    products(table, (p0, p1, p2, p3), right, acc)
    value = acc[...].astype(BF16)
    squared[...] = value
    mixed[...] = turn(value)


def purify(table, p0, p1, p2, p3, right, squared, acc):
    products(table, (p0, p1, p2, p3), right, acc)
    return (3.0 * squared[...].astype(F32) - 2.0 * acc[...]).astype(BF16)


def cube_kernel(table, p0, p1, p2, p3, right, squared, plain, mixed, acc):
    value = purify(table, p0, p1, p2, p3, right, squared, acc)
    plain[...] = value
    mixed[...] = turn(value)


def last_kernel(table, p0, p1, p2, p3, right, squared, out, acc):
    acc[...] = purify(table, p0, p1, p2, p3, right, squared, acc).astype(F32)
    for p in range(ROWS):
        out[:, 128 * p : 128 * (p + 1)] = acc[pl.ds(p, 16, stride=ROWS), :].astype(BF16)


def tag_kernel(pair, taken, other, tags):
    row = 0
    for part in (pair, taken, other):
        for at in range(WHOLE, part.shape[0], WHOLE + TAG):
            tags[row : row + 1, :] = part[at : at + TAG, :].astype(F32)[0:1, :].astype(jnp.int32)
            row += 1


def shape(rows, lanes=128):
    return jax.ShapeDtypeStruct((rows, lanes), BF16)


VMEM = pl.BlockSpec(memory_space=pltpu.VMEM)
SMEM = pl.BlockSpec(memory_space=pltpu.SMEM)


def call(kernel, outs, specs, more, args, scratch=True):
    return pl.pallas_call(
        kernel,
        out_shape=outs,
        in_specs=specs,
        out_specs=[VMEM] * len(outs),
        scratch_shapes=([pltpu.VMEM((WHOLE, 128), F32)] if scratch else []) + more,
        compiler_params=pltpu.CompilerParams(vmem_limit_bytes=8 * 1024 * 1024),
        cost_estimate=pl.CostEstimate(flops=2**31, bytes_accessed=2**21, transcendentals=0),
    )(*args)


def multiply(kernel, outs, table, pieces, *others):
    specs = [SMEM] + [VMEM] * (4 + len(others))
    return call(kernel, outs, specs, [], (table, *pieces, *others))


def match_table(columns, pieces, right):
    block = [p.reshape(4, WHOLE + TAG, 128)[:, WHOLE, :16] for p in pieces]
    place = place_of(jnp.concatenate(block, axis=0).astype(jnp.int32))
    outs = [jax.ShapeDtypeStruct((16, 128), jnp.int32)]
    (tags,) = call(tag_kernel, outs, [VMEM] * 3, [], right, False)
    listed = tags[:, :16].reshape(256)
    hit = place[..., None] == jnp.arange(256, dtype=jnp.int32)
    there = jnp.sum(jnp.where(hit, listed, 0), axis=2)
    found = jnp.where(there == columns, place, -1)
    most = jnp.max(found, axis=1, keepdims=True)
    count = jnp.sum((most >= 0).astype(jnp.int32).reshape(4, 4), axis=1, keepdims=True)
    count = jnp.broadcast_to(count, (4, 4)).reshape(16, 1)
    return jnp.concatenate([found, most, count], axis=1)


def body(density, columns):
    columns = columns.reshape(1, 16)
    plain, mixed = call(
        prepare_kernel,
        [shape(WHOLE + TAG)] * 2,
        [VMEM, VMEM],
        [pltpu.VMEM((TAG, 128), F32)],
        (density.reshape(16, 4096), columns),
    )
    table = None
    for step in range(STEPS):
        pieces, parts = gather_both(plain, mixed)
        if table is None:
            table = match_table(columns, pieces, parts)
        outs = [shape(16 * WHOLE), shape(WHOLE), shape(WHOLE)]
        right, squared, mixed = multiply(square_kernel, outs, table, pieces, *parts)
        pieces = gather_left(mixed)
        if step < STEPS - 1:
            plain, mixed = multiply(cube_kernel, outs[1:], table, pieces, right, squared)
    (out,) = multiply(last_kernel, [shape(16, 4096)], table, pieces, right, squared)
    return out.reshape(16, 1, 4096)


def solution(mesh):
    placed = (P("row", "col", None), P("row", "col"))
    return jax.shard_map(
        body, mesh=mesh, in_specs=placed, out_specs=P("row", "col", None), check_vma=False
    )
```

```python
import jax
import jax.numpy as jnp
from jax import lax
from jax.experimental import pallas as pl
from jax.experimental.pallas import tpu as pltpu
from jax.sharding import PartitionSpec as P

STEPS = 2
SIDE = 64
ROWS = 32
CHUNK = 16
TAG = 16
WHOLE = 16 * ROWS
BF16 = jnp.bfloat16
F32 = jnp.float32


def shift(first, d):
    pairs = []
    for row in range(16):
        for y in range(4):
            for x in range(4):
                along_x = (row % 2 == 0) == first
                to = (y, (x + d) % 4) if along_x else ((y + d) % 4, x)
                pairs.append((row * 16 + y * 4 + x, row * 16 + to[0] * 4 + to[1]))
    return pairs


def gather_left(own):
    near = [own] + [lax.ppermute(own, ("row", "col"), shift(True, d)) for d in (1, 3, 2)]
    near = jnp.concatenate(near, axis=0)
    return [near] + [lax.ppermute(near, ("row", "col"), shift(False, d)) for d in (1, 3, 2)]


def shift_z(d):
    pairs = []
    for row in range(16):
        up = d if row % 2 == 0 else -d
        to = (row // 2 + up) % 8 * 2 + row % 2
        pairs += [(row * 16 + c, to * 16 + c) for c in range(16)]
    return pairs


OTHER_CORE = [(row * 16 + c, (row ^ 1) * 16 + c) for row in range(16) for c in range(16)]


def join_kernel(one, two, own, a, b, c, near, second, half, taken):
    rows = own.shape[0]
    for i, part in enumerate((own, a, b, c)):
        near[i * rows : (i + 1) * rows, :] = part[...]
    second[...] = two[...]
    half[...] = two[:rows, :]
    taken[: 2 * rows, :] = one[...]
    taken[2 * rows :, :] = two[...]


def taken_kernel(pair, first, three, four, taken, *tags):
    at = 0
    for part in (first, three, four):
        taken[at : at + part.shape[0], :] = part[...]
        at += part.shape[0]
    if tags:
        note, tag = tags[1], tags[0]
        note[...] = jnp.zeros_like(note)
        for i in range(9):
            ref, row = (taken, i) if i < 7 else (pair, i - 7)
            row = row * (WHOLE + TAG) + WHOLE
            to = i if i < 7 else i + 1
            note[to : to + 1, :] = ref[row : row + TAG, :].astype(F32)[0:1, :]
        tag[...] = note[...].astype(BF16)
        taken[at:, :] = tag[...]


def gather_both(plain, mixed):
    def send(value, pairs):
        return lax.ppermute(value, ("row", "col"), pairs)

    rows = plain.shape[0]
    near = [send(mixed, shift(True, d)) for d in (1, 3, 2)]
    pair = jnp.concatenate([plain, send(plain, OTHER_CORE)], axis=0)
    one, two = send(pair, shift_z(1)), send(pair, shift_z(2))
    near, two, half, taken = call(
        join_kernel,
        [shape(4 * rows), shape(2 * rows), shape(rows), shape(4 * rows)],
        [VMEM] * 6,
        [],
        (one, two, mixed, *near),
        False,
    )
    pieces = [near] + [send(near, shift(False, d)) for d in (1, 3, 2)]
    three, four = send(two, shift_z(1)), send(half, shift_z(2))
    three, four, *pieces[1:] = lax.optimization_barrier((three, four, *pieces[1:]))
    args = (pair, taken, three, four)
    if rows > WHOLE:
        outs, note = [shape(7 * rows + TAG), shape(TAG)], [pltpu.VMEM((TAG, 128), F32)]
        taken, tag = call(taken_kernel, outs, [VMEM] * 4, note, args, False)
    else:
        (taken,), tag = call(taken_kernel, [shape(7 * rows)], [VMEM] * 4, [], args, False), None
    other = send(taken, OTHER_CORE)
    right = (pair, taken, other)
    if tag is not None:
        tag = jnp.concatenate([tag[8:10], tag[:7], other[7 * rows : 7 * rows + 7]], axis=0)
    return pieces, right, tag


def place_of(block):
    row = lax.axis_index("row")
    z, core = row // 2, row % 2
    group = block // 16
    other = (group % 2 != core).astype(jnp.int32)
    far = jnp.where(core == 0, z - group // 2, group // 2 - z) % 8
    panel = jnp.where(
        far == 0,
        other,
        jnp.where(
            far < 4,
            2 * far + other,
            jnp.where(far == 4, 8 + 7 * other, 9 + 2 * (7 - far) + 1 - other),
        ),
    )
    return panel * 16 + block % 16


def turn(value):
    at = lax.broadcasted_iota(jnp.int32, (128, 128), 0)
    to = lax.broadcasted_iota(jnp.int32, (128, 128), 1)
    place = at // 64 * 64 + at % 2 * 32 + at % 64 // 2
    shuffle = (place == to).astype(F32).astype(BF16)
    return jnp.dot(value, shuffle, preferred_element_type=F32).astype(BF16)


def prepare_kernel(density, columns, plain, mixed, blocks, note):
    wide = density[...].astype(F32)
    for p in range(ROWS):
        blocks[pl.ds(p, 16, stride=ROWS), :] = wide[:, 128 * p : 128 * (p + 1)]
    value = blocks[...].astype(BF16)
    note[...] = jnp.zeros_like(note)
    note[0:1, 0:16] = columns[...].astype(F32)
    tag = note[...].astype(BF16)
    plain[:WHOLE, :] = value
    plain[WHOLE:, :] = tag
    mixed[:WHOLE, :] = turn(value)
    mixed[WHOLE:, :] = tag


def products(table, pieces, right, acc, groups=range(4)):
    step = pieces[0].shape[0] // 4
    if 0 in groups:
        acc[...] = jnp.zeros_like(acc)
    low = lax.broadcasted_iota(jnp.int32, (ROWS, 128), 1) < SIDE
    zero = jnp.zeros((ROWS, 128), BF16)

    def weights(s, i):
        at = table[s, i]
        row = pl.multiple_of(jnp.maximum(at, 0) * ROWS, 16)
        block = jnp.where(at >= 0, right[pl.ds(row, ROWS), :], zero)
        turned = jnp.concatenate([block[:, SIDE:], block[:, :SIDE]], axis=1)
        return [
            jnp.where(low, block, zero),
            jnp.where(low, turned, zero),
            jnp.where(low, zero, turned),
            jnp.where(low, zero, block),
        ]

    def add(g, places):
        def some(j, carry):
            for u in range(CHUNK):
                i = j * CHUNK + u
                rows = [pl.multiple_of(t * step + i * ROWS, 16) for t in places]
                a = [pieces[g][pl.ds(row, ROWS), :] for row in rows]
                b = [w for t in places for w in weights(4 * g + t, i)]
                a = a[0] if len(a) == 1 else jnp.concatenate(a, axis=1)
                out = pl.ds(pl.multiple_of(i * ROWS, 16), ROWS)
                acc[out, :] += jnp.dot(a, jnp.concatenate(b, axis=0), preferred_element_type=F32)
            return carry

        lax.fori_loop(0, 16 // CHUNK, some, 0)

    for g in groups:
        count = table[4 * g, 17]

        @pl.when(count > 1)
        def _(g=g):
            add(g, range(4))

        @pl.when(count == 1)
        def _(g=g):
            def one(t, carry):
                @pl.when(table[4 * g + t, 16] >= 0)
                def _():
                    add(g, [t])

                return carry

            lax.fori_loop(0, 4, one, 0)


def square_kernel(table, p0, p1, p2, p3, pair, taken, other, right, squared, mixed, acc):
    panel = pair.shape[0] // 2
    place = 0
    for part in (pair, taken, other):
        for at in range(0, part.shape[0] // panel * panel, panel):
            right[place : place + WHOLE, :] = part[at : at + WHOLE, :]
            place += WHOLE
    products(table, (p0, p1, p2, p3), right, acc)
    value = acc[...].astype(BF16)
    squared[...] = value
    mixed[...] = turn(value)


def near_kernel(table, p0, right, acc):
    products(table, (p0,), right, acc, range(1))


def purify(table, p1, p2, p3, right, squared, near, acc):
    acc[...] = near[...]
    products(table, (p1, p1, p2, p3), right, acc, range(1, 4))
    return (3.0 * squared[...].astype(F32) - 2.0 * acc[...]).astype(BF16)


def cube_kernel(table, p1, p2, p3, right, squared, near, plain, mixed, acc):
    value = purify(table, p1, p2, p3, right, squared, near, acc)
    plain[...] = value
    mixed[...] = turn(value)


def last_kernel(table, p1, p2, p3, right, squared, near, out, acc):
    acc[...] = purify(table, p1, p2, p3, right, squared, near, acc).astype(F32)
    for p in range(ROWS):
        out[:, 128 * p : 128 * (p + 1)] = acc[pl.ds(p, 16, stride=ROWS), :].astype(BF16)


def shape(rows, lanes=128):
    return jax.ShapeDtypeStruct((rows, lanes), BF16)


VMEM = pl.BlockSpec(memory_space=pltpu.VMEM)
SMEM = pl.BlockSpec(memory_space=pltpu.SMEM)


def call(kernel, outs, specs, more, args, scratch=True):
    return pl.pallas_call(
        kernel,
        out_shape=outs,
        in_specs=specs,
        out_specs=[VMEM] * len(outs),
        scratch_shapes=([pltpu.VMEM((WHOLE, 128), F32)] if scratch else []) + more,
        compiler_params=pltpu.CompilerParams(vmem_limit_bytes=8 * 1024 * 1024),
        cost_estimate=pl.CostEstimate(flops=2**31, bytes_accessed=2**21, transcendentals=0),
    )(*args)


def multiply(kernel, outs, table, pieces, *others):
    specs = [SMEM] + [VMEM] * (len(pieces) + len(others))
    return call(kernel, outs, specs, [], (table, *pieces, *others))


def match_table(columns, pieces, tag):
    block = [p.reshape(4, WHOLE + TAG, 128)[:, WHOLE, :16] for p in pieces]
    place = place_of(jnp.concatenate(block, axis=0).astype(jnp.int32))
    listed = tag[:, :16].astype(jnp.int32).reshape(256)
    hit = place[..., None] == jnp.arange(256, dtype=jnp.int32)
    there = jnp.sum(jnp.where(hit, listed, 0), axis=2)
    found = jnp.where(there == columns, place, -1)
    most = jnp.max(found, axis=1, keepdims=True)
    count = jnp.sum((most >= 0).astype(jnp.int32).reshape(4, 4), axis=1, keepdims=True)
    count = jnp.broadcast_to(count, (4, 4)).reshape(16, 1)
    return jnp.concatenate([found, most, count], axis=1)


def body(density, columns):
    columns = columns.reshape(1, 16)
    plain, mixed = call(
        prepare_kernel,
        [shape(WHOLE + TAG)] * 2,
        [VMEM, VMEM],
        [pltpu.VMEM((TAG, 128), F32)],
        (density.reshape(16, 4096), columns),
    )
    table = None
    for step in range(STEPS):
        pieces, parts, tag = gather_both(plain, mixed)
        if table is None:
            table = match_table(columns, pieces, tag)
        outs = [shape(16 * WHOLE), shape(WHOLE), shape(WHOLE)]
        right, squared, mixed = multiply(square_kernel, outs, table, pieces, *parts)
        pieces = gather_left(mixed)
        args, specs = (table, pieces[0], right), [SMEM, VMEM, VMEM]
        sums = [jax.ShapeDtypeStruct((WHOLE, 128), F32)]
        (near,) = call(near_kernel, sums, specs, [], args, False)
        if step < STEPS - 1:
            plain, mixed = multiply(cube_kernel, outs[1:], table, pieces[1:], right, squared, near)
    (out,) = multiply(last_kernel, [shape(16, 4096)], table, pieces[1:], right, squared, near)
    return out.reshape(16, 1, 4096)


def solution(mesh):
    placed = (P("row", "col", None), P("row", "col"))
    return jax.shard_map(
        body, mesh=mesh, in_specs=placed, out_specs=P("row", "col", None), check_vma=False
    )
```

```python
import jax
import jax.numpy as jnp
from jax import lax
from jax.experimental import pallas as pl
from jax.experimental.pallas import tpu as pltpu
from jax.sharding import PartitionSpec as P

STEPS = 2
SIDE = 64
ROWS = 32
CHUNK = 16
TAG = 16
WHOLE = 16 * ROWS
BF16 = jnp.bfloat16
F32 = jnp.float32


def shift(first, d):
    pairs = []
    for row in range(16):
        for y in range(4):
            for x in range(4):
                along_x = (row % 2 == 0) == first
                to = (y, (x + d) % 4) if along_x else ((y + d) % 4, x)
                pairs.append((row * 16 + y * 4 + x, row * 16 + to[0] * 4 + to[1]))
    return pairs


def gather_left(own):
    near = [own] + [lax.ppermute(own, ("row", "col"), shift(True, d)) for d in (1, 3, 2)]
    near = jnp.concatenate(near, axis=0)
    return [near] + [lax.ppermute(near, ("row", "col"), shift(False, d)) for d in (1, 3, 2)]


def shift_z(d):
    pairs = []
    for row in range(16):
        up = d if row % 2 == 0 else -d
        to = (row // 2 + up) % 8 * 2 + row % 2
        pairs += [(row * 16 + c, to * 16 + c) for c in range(16)]
    return pairs


OTHER_CORE = [(row * 16 + c, (row ^ 1) * 16 + c) for row in range(16) for c in range(16)]


def join_kernel(one, two, own, a, b, c, near, second, half, taken):
    rows = own.shape[0]
    for i, part in enumerate((own, a, b, c)):
        near[i * rows : (i + 1) * rows, :] = part[...]
    second[...] = two[...]
    half[...] = two[:rows, :]
    taken[: 2 * rows, :] = one[...]
    taken[2 * rows :, :] = two[...]


def taken_kernel(pair, first, three, four, taken, *tags):
    at = 0
    for part in (first, three, four):
        taken[at : at + part.shape[0], :] = part[...]
        at += part.shape[0]
    if tags:
        note, tag = tags[1], tags[0]
        note[...] = jnp.zeros_like(note)
        for i in range(9):
            ref, row = (taken, i) if i < 7 else (pair, i - 7)
            row = row * (WHOLE + TAG) + WHOLE
            to = i if i < 7 else i + 1
            note[to : to + 1, :] = ref[row : row + TAG, :].astype(F32)[0:1, :]
        tag[...] = note[...].astype(BF16)
        taken[at:, :] = tag[...]


def gather_both(plain, mixed):
    def send(value, pairs):
        return lax.ppermute(value, ("row", "col"), pairs)

    rows = plain.shape[0]
    near = [send(mixed, shift(True, d)) for d in (1, 3, 2)]
    pair = jnp.concatenate([plain, send(plain, OTHER_CORE)], axis=0)
    one, two = send(pair, shift_z(1)), send(pair, shift_z(2))
    near, two, half, taken = call(
        join_kernel,
        [shape(4 * rows), shape(2 * rows), shape(rows), shape(4 * rows)],
        [VMEM] * 6,
        [],
        (one, two, mixed, *near),
        False,
    )
    pieces = [near] + [send(near, shift(False, d)) for d in (1, 3, 2)]
    three, four = send(two, shift_z(1)), send(half, shift_z(2))
    first = 3 if rows > WHOLE else 1
    three, four, *pieces[first:] = lax.optimization_barrier((three, four, *pieces[first:]))
    args = (pair, taken, three, four)
    if rows > WHOLE:
        outs, note = [shape(7 * rows + TAG), shape(TAG)], [pltpu.VMEM((TAG, 128), F32)]
        taken, tag = call(taken_kernel, outs, [VMEM] * 4, note, args, False)
    else:
        (taken,), tag = call(taken_kernel, [shape(7 * rows)], [VMEM] * 4, [], args, False), None
    other = send(taken, OTHER_CORE)
    right = (pair, taken, other)
    if tag is not None:
        tag = jnp.concatenate([tag[8:10], tag[:7], other[7 * rows : 7 * rows + 7]], axis=0)
    return pieces, right, tag


def place_of(block):
    row = lax.axis_index("row")
    z, core = row // 2, row % 2
    group = block // 16
    other = (group % 2 != core).astype(jnp.int32)
    far = jnp.where(core == 0, z - group // 2, group // 2 - z) % 8
    panel = jnp.where(
        far == 0,
        other,
        jnp.where(
            far < 4,
            2 * far + other,
            jnp.where(far == 4, 8 + 7 * other, 9 + 2 * (7 - far) + 1 - other),
        ),
    )
    return panel * 16 + block % 16


def turn(value):
    at = lax.broadcasted_iota(jnp.int32, (128, 128), 0)
    to = lax.broadcasted_iota(jnp.int32, (128, 128), 1)
    place = at // 64 * 64 + at % 2 * 32 + at % 64 // 2
    shuffle = (place == to).astype(F32).astype(BF16)
    return jnp.dot(value, shuffle, preferred_element_type=F32).astype(BF16)


def prepare_kernel(density, columns, plain, mixed, blocks, note):
    wide = density[...].astype(F32)
    for p in range(ROWS):
        blocks[pl.ds(p, 16, stride=ROWS), :] = wide[:, 128 * p : 128 * (p + 1)]
    value = blocks[...].astype(BF16)
    note[...] = jnp.zeros_like(note)
    note[0:1, 0:16] = columns[...].astype(F32)
    tag = note[...].astype(BF16)
    plain[:WHOLE, :] = value
    plain[WHOLE:, :] = tag
    mixed[:WHOLE, :] = turn(value)
    mixed[WHOLE:, :] = tag


def products(table, pieces, right, acc, groups=range(4)):
    step = pieces[0].shape[0] // 4
    if 0 in groups:
        acc[...] = jnp.zeros_like(acc)
    low = lax.broadcasted_iota(jnp.int32, (ROWS, 128), 1) < SIDE
    zero = jnp.zeros((ROWS, 128), BF16)

    def weights(s, i):
        at = table[s, i]
        row = pl.multiple_of(jnp.maximum(at, 0) * ROWS, 16)
        block = jnp.where(at >= 0, right[pl.ds(row, ROWS), :], zero)
        turned = jnp.concatenate([block[:, SIDE:], block[:, :SIDE]], axis=1)
        return [
            jnp.where(low, block, zero),
            jnp.where(low, turned, zero),
            jnp.where(low, zero, turned),
            jnp.where(low, zero, block),
        ]

    def add(g, places):
        def some(j, carry):
            for u in range(CHUNK):
                i = j * CHUNK + u
                rows = [pl.multiple_of(t * step + i * ROWS, 16) for t in places]
                a = [pieces[g][pl.ds(row, ROWS), :] for row in rows]
                b = [w for t in places for w in weights(4 * g + t, i)]
                a = a[0] if len(a) == 1 else jnp.concatenate(a, axis=1)
                out = pl.ds(pl.multiple_of(i * ROWS, 16), ROWS)
                acc[out, :] += jnp.dot(a, jnp.concatenate(b, axis=0), preferred_element_type=F32)
            return carry

        lax.fori_loop(0, 16 // CHUNK, some, 0)

    for g in groups:
        count = table[4 * g, 17]

        @pl.when(count > 1)
        def _(g=g):
            add(g, range(4))

        @pl.when(count == 1)
        def _(g=g):
            def one(t, carry):
                @pl.when(table[4 * g + t, 16] >= 0)
                def _():
                    add(g, [t])

                return carry

            lax.fori_loop(0, 4, one, 0)


def square_kernel(table, p0, p1, p2, p3, pair, taken, other, right, squared, mixed, acc):
    panel = pair.shape[0] // 2
    place = 0
    for part in (pair, taken, other):
        for at in range(0, part.shape[0] // panel * panel, panel):
            right[place : place + WHOLE, :] = part[at : at + WHOLE, :]
            place += WHOLE
    products(table, (p0, p1, p2, p3), right, acc)
    value = acc[...].astype(BF16)
    squared[...] = value
    mixed[...] = turn(value)


def near_kernel(table, p0, right, acc):
    products(table, (p0,), right, acc, range(1))


def purify(table, p1, p2, p3, right, squared, near, acc):
    acc[...] = near[...]
    products(table, (p1, p1, p2, p3), right, acc, range(1, 4))
    return (3.0 * squared[...].astype(F32) - 2.0 * acc[...]).astype(BF16)


def cube_kernel(table, p1, p2, p3, right, squared, near, plain, mixed, acc):
    value = purify(table, p1, p2, p3, right, squared, near, acc)
    plain[...] = value
    mixed[...] = turn(value)


def last_kernel(table, p1, p2, p3, right, squared, near, out, acc):
    acc[...] = purify(table, p1, p2, p3, right, squared, near, acc).astype(F32)
    for p in range(ROWS):
        out[:, 128 * p : 128 * (p + 1)] = acc[pl.ds(p, 16, stride=ROWS), :].astype(BF16)


def shape(rows, lanes=128):
    return jax.ShapeDtypeStruct((rows, lanes), BF16)


VMEM = pl.BlockSpec(memory_space=pltpu.VMEM)
SMEM = pl.BlockSpec(memory_space=pltpu.SMEM)


def call(kernel, outs, specs, more, args, scratch=True):
    return pl.pallas_call(
        kernel,
        out_shape=outs,
        in_specs=specs,
        out_specs=[VMEM] * len(outs),
        scratch_shapes=([pltpu.VMEM((WHOLE, 128), F32)] if scratch else []) + more,
        compiler_params=pltpu.CompilerParams(vmem_limit_bytes=8 * 1024 * 1024),
        cost_estimate=pl.CostEstimate(flops=2**31, bytes_accessed=2**21, transcendentals=0),
    )(*args)


def multiply(kernel, outs, table, pieces, *others):
    specs = [SMEM] + [VMEM] * (len(pieces) + len(others))
    return call(kernel, outs, specs, [], (table, *pieces, *others))


def match_table(columns, pieces, tag):
    block = [p.reshape(4, WHOLE + TAG, 128)[:, WHOLE, :16] for p in pieces]
    place = place_of(jnp.concatenate(block, axis=0).astype(jnp.int32))
    listed = tag[:, :16].astype(jnp.int32).reshape(256)
    hit = place[..., None] == jnp.arange(256, dtype=jnp.int32)
    there = jnp.sum(jnp.where(hit, listed, 0), axis=2)
    found = jnp.where(there == columns, place, -1)
    most = jnp.max(found, axis=1, keepdims=True)
    count = jnp.sum((most >= 0).astype(jnp.int32).reshape(4, 4), axis=1, keepdims=True)
    count = jnp.broadcast_to(count, (4, 4)).reshape(16, 1)
    return jnp.concatenate([found, most, count], axis=1)


def body(density, columns):
    columns = columns.reshape(1, 16)
    plain, mixed = call(
        prepare_kernel,
        [shape(WHOLE + TAG)] * 2,
        [VMEM, VMEM],
        [pltpu.VMEM((TAG, 128), F32)],
        (density.reshape(16, 4096), columns),
    )
    table = None
    for step in range(STEPS):
        pieces, parts, tag = gather_both(plain, mixed)
        if table is None:
            table = match_table(columns, pieces, tag)
        outs = [shape(16 * WHOLE), shape(WHOLE), shape(WHOLE)]
        right, squared, mixed = multiply(square_kernel, outs, table, pieces, *parts)
        pieces = gather_left(mixed)
        args, specs = (table, pieces[0], right), [SMEM, VMEM, VMEM]
        sums = [jax.ShapeDtypeStruct((WHOLE, 128), F32)]
        (near,) = call(near_kernel, sums, specs, [], args, False)
        if step < STEPS - 1:
            plain, mixed = multiply(cube_kernel, outs[1:], table, pieces[1:], right, squared, near)
    (out,) = multiply(last_kernel, [shape(16, 4096)], table, pieces[1:], right, squared, near)
    return out.reshape(16, 1, 4096)


def solution(mesh):
    placed = (P("row", "col", None), P("row", "col"))
    return jax.shard_map(
        body, mesh=mesh, in_specs=placed, out_specs=P("row", "col", None), check_vma=False
    )
```
